32 devices in a mesh: chan: 16 (over z, x, core), win: 2 (over y).
Axes of the slice: x: 2, y: 2, z: 4, core: 2. Of those that a mesh axis runs over, the one named last changes fastest.
Arguments:
- spectra: bfloat16 [2, 4, 2048, 4096], P(None, 'win', 'chan'), may hold values from -6 to 6
- exponents: int32 [4, 2048, 32], P('win', 'chan'), may hold values from -1 to 1
- source_channels: int32 [1], replicated, may hold values from 0 to 2047
Outputs:
- correlations: float32 [1, 2048, 2048], P(None, 'chan', 'win')
The draws below stay inside these ranges and needn't reach their ends.
All inputs are finite; a program needn't handle non-finite values.
Results may differ from the reference program's by a relative error of at most 0.0003.
Values sent between devices are 32-bit elements; how exact they have to be, the bound alone decides.
A program may use at most 64 MiB of HBM per device.

```python
import math
import jax
import jax.numpy as jnp
from jax import lax

F = 4096
L = 2048
BLK = 128
S = 1
C = 2048
NSEG = 4


def touch_ends(array, rng, least, top_value):
    dims = array.shape
    place = [jax.random.randint(jax.random.fold_in(rng, axis), (), 0, dims[axis]) for axis in range(len(dims))]
    array = array.at[tuple(place)].set(least)
    longest = dims.index(max(dims))
    place[longest] = (place[longest] + 1) % dims[longest]
    return array.at[tuple(place)].set(top_value)


def block_scale(stream_key, shape, cuts, low, top_value):
    def one(position, blocks):
        heights = jax.random.uniform(jax.random.fold_in(jax.random.fold_in(stream_key, 6), position), (blocks,), jnp.float32, low / len(cuts), top_value / len(cuts))
        return jnp.repeat(jnp.exp(heights), shape[position] // blocks).reshape((-1,) + (1,) * (len(shape) - position - 1))

    loudness = one(*cuts[0])
    for cut in cuts[1:]:
        loudness = loudness * one(*cut)
    return loudness


def gaussian(rng, dims, scale, most, cuts=(), dtype=jnp.bfloat16):
    drawn = scale * jax.random.normal(rng, dims, jnp.float32)
    if cuts:
        drawn = drawn * block_scale(rng, dims, cuts, -0.22, 0.18)
    return jnp.clip(drawn, -most, most).astype(dtype)


def setup_inputs(seed: int = 0) -> dict:
    keys = jax.random.split(jax.random.key(seed), 4)
    spectra = gaussian(keys[0], (2, NSEG, C, F), 1.0, 6.0, ((1, 2), (2, 16)))
    exponents = touch_ends(jax.random.randint(keys[1], (NSEG, C, F // BLK), -1, 2), jax.random.fold_in(keys[1], 1), -1, 1).astype(jnp.int32)
    source_channels = jax.random.randint(keys[2], (S,), 0, C).astype(jnp.int32)
    return dict(spectra=spectra, exponents=exponents, source_channels=source_channels)


def dequantize(spectra, exponents):
    scale = jnp.exp2(exponents.astype(jnp.float32))
    scale = jnp.repeat(scale, BLK, axis=2)
    return spectra.astype(jnp.float32) * scale[None]

def reference(spectra, exponents, source_channels):
    values = dequantize(spectra, exponents)
    slab = jnp.take(values, source_channels.astype(jnp.int32), axis=2)
    high = lax.Precision.HIGHEST
    real_part = jnp.einsum('gsf,gcf->scf', slab[0], values[0], precision=high) + jnp.einsum('gsf,gcf->scf', slab[1], values[1], precision=high)
    imag_part = jnp.einsum('gsf,gcf->scf', slab[0], values[1], precision=high) - jnp.einsum('gsf,gcf->scf', slab[1], values[0], precision=high)
    padded_real = jnp.concatenate([real_part, jnp.zeros_like(real_part)], axis=2)
    padded_imag = jnp.concatenate([imag_part, jnp.zeros_like(imag_part)], axis=2)
    spectrum = padded_real + 1j * padded_imag
    period = 2 * F
    inverse = jnp.real(jnp.fft.ifft(spectrum, axis=2)) * period
    lagged = jnp.concatenate([inverse[:, :, period - L // 2:], inverse[:, :, :L // 2]], axis=2)
    norm = 1.0 / math.sqrt(4.0 * F * NSEG)
    return lagged * norm
```

```python
import functools
import math

import jax
import jax.numpy as jnp
import ml_dtypes
import numpy as np
from jax import lax
from jax.experimental import pallas as pl
from jax.experimental.pallas import tpu as pltpu
from jax.sharding import PartitionSpec as P

L = 2048
FOLD = 8
CLASSES = 2 * FOLD
LANES = 128
PACK = 16
MESH = pl.DeviceIdType.MESH


def lag_tables(nbin, norm):
    width = nbin // FOLD
    steps = L // CLASSES
    tau = np.arange(CLASSES)[:, None] + CLASSES * (np.arange(steps) - steps // 2)[None, :]
    phase = (tau[:, :, None] * np.arange(width)[None, None, :]) % (2 * nbin)
    angle = phase * (2.0 * math.pi / (2 * nbin))
    full = np.concatenate([np.cos(angle), -np.sin(angle)], axis=2) * norm
    high = full.astype(np.float32).astype(ml_dtypes.bfloat16)
    low = (full - high.astype(np.float64)).astype(np.float32).astype(ml_dtypes.bfloat16)
    return np.concatenate([high, low], axis=1)


def turn(value, eighths):
    re, im = value
    k = eighths % 16
    if k == 0:
        return re, im
    if k == 4:
        return -im, re
    if k == 8:
        return -re, -im
    if k == 12:
        return im, -re
    if k == 2:
        c = math.sqrt(0.5)
        return (re - im) * c, (re + im) * c
    if k == 6:
        c = math.sqrt(0.5)
        return (re + im) * -c, (re - im) * c
    c, s = math.cos(math.pi * k / 8), math.sin(math.pi * k / 8)
    return re * c - im * s, re * s + im * c


def dft(values):
    n = len(values)
    if n == 1:
        return values
    even, odd = dft(values[0::2]), dft(values[1::2])
    odd = [turn(v, 16 // n * k) for k, v in enumerate(odd)]
    low = [(a[0] + b[0], a[1] + b[1]) for a, b in zip(even, odd)]
    high = [(a[0] - b[0], a[1] - b[1]) for a, b in zip(even, odd)]
    return low + high


def kernel(nch, nwin, src_ref, exp_ref, spec_hbm, tab_hbm, out_ref,
           spec, tab, pick, got, mine, slab, folded, part, come, acc,
           spec_sem, tab_sem, s1, r1, s2, r2, s3, r3):
    chan, win = lax.axis_index("chan"), lax.axis_index("win")
    segs, rows, nbin = spec.shape[1], spec.shape[2], spec.shape[3]
    blocks = nbin // LANES
    per = slab.shape[1]
    width = nbin // FOLD
    jblocks = width // LANES
    steps = L // CLASSES
    mine_steps = steps // nwin

    load = pltpu.make_async_copy(spec_hbm, spec, spec_sem)
    load.start()
    load_tab = pltpu.make_async_copy(tab_hbm, tab, tab_sem)
    load_tab.start()

    barrier = pltpu.get_barrier_semaphore()

    @pl.loop(1, nch)
    def _(d):
        pl.semaphore_signal(barrier, inc=1, device_id=(lax.rem(chan + d, nch), win), device_id_type=MESH)

    @pl.loop(1, nwin)
    def _(d):
        pl.semaphore_signal(barrier, inc=1, device_id=(chan, lax.rem(win + d, nwin)), device_id_type=MESH)

    load.wait()
    local = src_ref[0] - chan * rows
    line = lax.broadcasted_iota(jnp.int32, (rows, LANES), 0)
    hits = (line == local).astype(jnp.float32)
    groups = rows // PACK
    marks = [hits[i * PACK : (i + 1) * PACK].astype(jnp.bfloat16) for i in range(groups)]
    for g in range(segs):
        scale = jnp.sum(jnp.exp2(exp_ref[g].astype(jnp.float32)) * hits[:, :blocks], axis=0, keepdims=True)
        for b in range(blocks):
            wide = jnp.broadcast_to(scale[:, b : b + 1], (1, LANES))
            for plane in range(2):
                x = None
                for i in range(groups):
                    y = spec[plane, g, i * PACK : (i + 1) * PACK, b * LANES : (b + 1) * LANES] * marks[i]
                    x = y if x is None else x + y
                row = (plane * segs + g) * blocks + b
                one = jnp.sum(x.astype(jnp.float32), axis=0, keepdims=True)
                pick[row // per, row % per : row % per + 1, :] = one * wide

    pl.semaphore_wait(barrier, nch + nwin - 2)

    def scatter(d):
        to = lax.rem(chan + d, nch)
        return pltpu.make_async_remote_copy(
            src_ref=pick.at[to], dst_ref=got.at[d], send_sem=s1.at[d], recv_sem=r1.at[d],
            device_id=(to, win), device_id_type=MESH)

    def gather(d):
        to = lax.rem(chan + d, nch)
        return pltpu.make_async_remote_copy(
            src_ref=mine, dst_ref=slab.at[chan], send_sem=s2.at[d], recv_sem=r2.at[d],
            device_id=(to, win), device_id_type=MESH)

    @pl.loop(1, nch)
    def _(d):
        scatter(d).start()

    total = pick[chan]
    for d in range(1, nch):
        scatter(d).wait_recv()
        total = total + got[d]
    mine[...] = total
    slab[chan] = total

    @pl.loop(1, nch)
    def _(d):
        gather(d).start()

    @pl.loop(0, rows // PACK)
    def _(i):
        here = pl.ds(pl.multiple_of(i * PACK, PACK), PACK)
        for g in range(segs):
            scale = jnp.exp2(exp_ref[g, here, :].astype(jnp.float32))
            for b in range(blocks):
                wide = jnp.broadcast_to(scale[:, b : b + 1], (PACK, LANES))
                cut = slice(b * LANES, (b + 1) * LANES)
                for plane in range(2):
                    x = spec[plane, g, here, cut].astype(jnp.float32)
                    spec[plane, g, here, cut] = (x * wide).astype(jnp.bfloat16)

    @pl.loop(1, nch)
    def _(d):
        gather(d).wait_recv()

    @pl.loop(0, rows // PACK)
    def _(i):
        start = pl.multiple_of(i * PACK, PACK)
        here = pl.ds(start, PACK)
        below = pl.ds(pl.multiple_of(rows + start, PACK), PACK)
        for j in range(jblocks):
            cross = []
            for h in range(FOLD):
                b = h * jblocks + j
                cut = slice(b * LANES, (b + 1) * LANES)
                re = im = None
                for g in range(segs):
                    ra, rb = g * blocks + b, (segs + g) * blocks + b
                    sr = slab[ra // per, ra % per : ra % per + 1, :]
                    si = slab[rb // per, rb % per : rb % per + 1, :]
                    xr = spec[0, g, here, cut].astype(jnp.float32)
                    xi = spec[1, g, here, cut].astype(jnp.float32)
                    tr, ti = sr * xr + si * xi, sr * xi - si * xr
                    re, im = (tr, ti) if re is None else (re + tr, im + ti)
                cross.append((re, im))
            for odd in range(2):
                if odd:
                    cross = [turn(v, h) for h, v in enumerate(cross)]
                for m, pair in enumerate(dft(cross)):
                    for plane in range(2):
                        cut = slice(plane * width + j * LANES, plane * width + (j + 1) * LANES)
                        high = pair[plane].astype(jnp.bfloat16)
                        low = (pair[plane] - high.astype(jnp.float32)).astype(jnp.bfloat16)
                        folded[2 * m + odd, here, cut] = high
                        folded[2 * m + odd, below, cut] = low

    load_tab.wait()

    def give(k, d):
        to = lax.rem(win + d, nwin)
        return pltpu.make_async_remote_copy(
            src_ref=part.at[k, to], dst_ref=come.at[d - 1, k], send_sem=s3.at[k, d - 1],
            recv_sem=r3.at[k, d - 1], device_id=(chan, to), device_id_type=MESH)

    @pl.loop(0, CLASSES)
    def _(k):
        r = lax.dot_general(tab[k], folded[k], (((1,), (1,)), ((), ())),
                            preferred_element_type=jnp.float32)
        low = r[:steps, rows:] + r[steps:, :rows] + r[steps:, rows:]
        part[k] = (r[:steps, :rows] + low).reshape(nwin, mine_steps, rows)
        for d in range(1, nwin):
            give(k, d).start()

    @pl.loop(1, nch)
    def _(d):
        scatter(d).wait_send()
        gather(d).wait_send()

    for k in range(CLASSES):
        value = part[k, win]
        for d in range(1, nwin):
            give(k, d).wait_recv()
            value = value + come[d - 1, k]
        acc[pl.ds(k, mine_steps, stride=CLASSES), :] = value

    for t in range(L // nwin // LANES):
        cut = slice(t * LANES, (t + 1) * LANES)
        out_ref[:, cut] = acc[cut, :].T

    @pl.loop(0, CLASSES)
    def _(k):
        for d in range(1, nwin):
            give(k, d).wait_send()


def body(spectra, exponents, source_channels):
    nch, nwin = lax.axis_size("chan"), lax.axis_size("win")
    _, segs, rows, nbin = spectra.shape
    per = 2 * segs * nbin // LANES // nch
    steps = L // CLASSES
    width = nbin // FOLD
    tables = jnp.asarray(lag_tables(nbin, 1.0 / math.sqrt(4.0 * nbin * segs * nwin)))
    f32, bf16, dma = jnp.float32, jnp.bfloat16, pltpu.SemaphoreType.DMA
    call = pl.pallas_call(
        functools.partial(kernel, nch, nwin),
        out_shape=jax.ShapeDtypeStruct((rows, L // nwin), f32),
        in_specs=[
            pl.BlockSpec(memory_space=pltpu.SMEM),
            pl.BlockSpec(memory_space=pltpu.VMEM),
            pl.BlockSpec(memory_space=pl.ANY),
            pl.BlockSpec(memory_space=pl.ANY),
        ],
        out_specs=pl.BlockSpec(memory_space=pltpu.VMEM),
        scratch_shapes=[
            pltpu.VMEM(spectra.shape, bf16),
            pltpu.VMEM((CLASSES, 2 * steps, 2 * width), bf16),
            pltpu.VMEM((nch, per, LANES), f32),
            pltpu.VMEM((nch, per, LANES), f32),
            pltpu.VMEM((per, LANES), f32),
            pltpu.VMEM((nch, per, LANES), f32),
            pltpu.VMEM((CLASSES, 2 * rows, 2 * width), bf16),
            pltpu.VMEM((CLASSES, nwin, steps // nwin, rows), f32),
            pltpu.VMEM((nwin - 1, CLASSES, steps // nwin, rows), f32),
            pltpu.VMEM((L // nwin, rows), f32),
            dma, dma,
            dma((nch,)), dma((nch,)), dma((nch,)), dma((nch,)),
            dma((CLASSES, nwin - 1)), dma((CLASSES, nwin - 1)),
        ],
        compiler_params=pltpu.CompilerParams(
            collective_id=0, has_side_effects=True, vmem_limit_bytes=48 * 2**20),
    )
    out = [call(source_channels[s : s + 1], exponents, spectra, tables)
           for s in range(source_channels.shape[0])]
    return jnp.stack(out)


def solution(mesh):
    return jax.shard_map(
        body,
        mesh=mesh,
        in_specs=(P(None, "win", "chan", None), P("win", "chan", None), P()),
        out_specs=P(None, "chan", "win"),
        check_vma=False,
    )
```

```python
import functools
import math

import jax
import jax.numpy as jnp
import ml_dtypes
import numpy as np
from jax import lax
from jax.experimental import pallas as pl
from jax.experimental.pallas import tpu as pltpu
from jax.sharding import PartitionSpec as P

L = 2048
FOLD = 8
CLASSES = 2 * FOLD
LANES = 128
PACK = 16
NEAR = 4
MESH = pl.DeviceIdType.MESH


def lag_tables(nbin, norm):
    width = nbin // FOLD
    steps = L // CLASSES
    tau = np.arange(CLASSES)[:, None] + CLASSES * (np.arange(steps) - steps // 2)[None, :]
    phase = (tau[:, :, None] * np.arange(width)[None, None, :]) % (2 * nbin)
    angle = phase * (2.0 * math.pi / (2 * nbin))
    full = np.concatenate([np.cos(angle), -np.sin(angle)], axis=2) * norm
    high = full.astype(np.float32).astype(ml_dtypes.bfloat16)
    low = (full - high.astype(np.float64)).astype(np.float32).astype(ml_dtypes.bfloat16)
    return np.concatenate([high, low], axis=1)


def turn(value, eighths):
    re, im = value
    k = eighths % 16
    if k == 0:
        return re, im
    if k == 4:
        return -im, re
    if k == 8:
        return -re, -im
    if k == 12:
        return im, -re
    if k == 2:
        c = math.sqrt(0.5)
        return (re - im) * c, (re + im) * c
    if k == 6:
        c = math.sqrt(0.5)
        return (re + im) * -c, (re - im) * c
    c, s = math.cos(math.pi * k / 8), math.sin(math.pi * k / 8)
    return re * c - im * s, re * s + im * c


def dft(values):
    n = len(values)
    if n == 1:
        return values
    even, odd = dft(values[0::2]), dft(values[1::2])
    odd = [turn(v, 16 // n * k) for k, v in enumerate(odd)]
    low = [(a[0] + b[0], a[1] + b[1]) for a, b in zip(even, odd)]
    high = [(a[0] - b[0], a[1] - b[1]) for a, b in zip(even, odd)]
    return low + high


def kernel(nch, nwin, src_ref, exp_hbm, spec_hbm, tab_hbm, out_ref,
           spec, tab, vals, raw, scales, pick, got, mine, got2, total, slab, even, odd,
           part, come, acc,
           spec_sem, tab_sem, exp_sem, s1, r1, s2, r2, s4, r4, s3, r3):
    chan, win = lax.axis_index("chan"), lax.axis_index("win")
    segs, rows, nbin = spec.shape[1], spec.shape[2], spec.shape[3]
    blocks = nbin // LANES
    per = slab.shape[1]
    width = nbin // FOLD
    jblocks = width // LANES
    steps = L // CLASSES
    mine_steps = steps // nwin

    load_exp = pltpu.make_async_copy(exp_hbm, raw, exp_sem)
    load_exp.start()
    load = pltpu.make_async_copy(spec_hbm, spec, spec_sem)
    load.start()
    load_tab = pltpu.make_async_copy(tab_hbm, tab, tab_sem)

    near, far = lax.rem(chan, NEAR), lax.div(chan, NEAR)
    nfar = nch // NEAR

    def beside(d):
        return lax.rem(near + d, NEAR)

    def ahead(d):
        return lax.rem(far + d, nfar) * NEAR + near

    barrier = pltpu.get_barrier_semaphore()
    for d in range(1, NEAR):
        pl.semaphore_signal(barrier, inc=1, device_id=(far * NEAR + beside(d), win), device_id_type=MESH)

    @pl.loop(1, nfar)
    def _(d):
        pl.semaphore_signal(barrier, inc=1, device_id=(ahead(d), win), device_id_type=MESH)

    @pl.loop(1, nwin)
    def _(d):
        pl.semaphore_signal(barrier, inc=1, device_id=(chan, lax.rem(win + d, nwin)), device_id_type=MESH)

    load_exp.wait()
    flat = jnp.exp2(raw[...].astype(jnp.float32)).reshape(segs * blocks, rows)
    square = jnp.concatenate([flat, jnp.ones((LANES - segs * blocks, rows), jnp.float32)], axis=0)
    scales[...] = square.T
    load.wait()
    load_tab.start()
    local = src_ref[0] - chan * rows
    line = lax.broadcasted_iota(jnp.int32, (rows, LANES), 0)
    hits = (line == local).astype(jnp.float32)
    groups = rows // PACK
    marks = [hits[i * PACK : (i + 1) * PACK].astype(jnp.bfloat16) for i in range(groups)]
    scale = jnp.sum(scales[...] * hits, axis=0, keepdims=True)
    for g in range(segs):
        for b in range(blocks):
            wide = jnp.broadcast_to(scale[:, g * blocks + b : g * blocks + b + 1], (1, LANES))
            for plane in range(2):
                x = None
                for i in range(groups):
                    y = spec[plane, g, i * PACK : (i + 1) * PACK, b * LANES : (b + 1) * LANES] * marks[i]
                    x = y if x is None else x + y
                row = (plane * segs + g) * blocks + b
                one = jnp.sum(x.astype(jnp.float32), axis=0, keepdims=True)
                pick[row // per, row % per : row % per + 1, :] = one * wide

    pl.semaphore_wait(barrier, NEAR + nfar + nwin - 3)

    def scatter(d):
        to = beside(d)
        return pltpu.make_async_remote_copy(
            src_ref=pick.at[to], dst_ref=got.at[d], send_sem=s1.at[d], recv_sem=r1.at[d],
            device_id=(far * NEAR + to, win), device_id_type=MESH)

    def across(d):
        return pltpu.make_async_remote_copy(
            src_ref=mine, dst_ref=got2.at[d], send_sem=s2.at[d], recv_sem=r2.at[d],
            device_id=(ahead(d), win), device_id_type=MESH)

    def gather(d):
        return pltpu.make_async_remote_copy(
            src_ref=total, dst_ref=slab.at[near], send_sem=s4.at[d], recv_sem=r4.at[d],
            device_id=(far * NEAR + beside(d), win), device_id_type=MESH)

    for d in range(1, NEAR):
        scatter(d).start()
    added = pick[near]
    for d in range(1, NEAR):
        scatter(d).wait_recv()
        added = added + got[d]
    mine[...] = added
    for d in range(1, nfar):
        across(d).start()

    @pl.loop(0, rows // PACK)
    def _(i):
        here = pl.ds(pl.multiple_of(i * PACK, PACK), PACK)
        scale = scales[here, :]
        for g in range(segs):
            for b in range(blocks):
                wide = jnp.broadcast_to(scale[:, g * blocks + b : g * blocks + b + 1], (PACK, LANES))
                cut = slice(b * LANES, (b + 1) * LANES)
                for plane in range(2):
                    x = spec[plane, g, here, cut].astype(jnp.float32)
                    vals[plane, g, here, cut] = x * wide

    for d in range(1, nfar):
        across(d).wait_recv()
        added = added + got2[d]
    total[...] = added
    slab[near] = added
    for d in range(1, NEAR):
        gather(d).start()
    for d in range(1, NEAR):
        gather(d).wait_recv()

    def split(folded, pairs, j, here, below):
        for m, pair in enumerate(dft(pairs)):
            for plane in range(2):
                cut = slice(plane * width + j * LANES, plane * width + (j + 1) * LANES)
                high = pair[plane].astype(jnp.bfloat16)
                low = (pair[plane] - high.astype(jnp.float32)).astype(jnp.bfloat16)
                folded[m, here, cut] = high
                folded[m, below, cut] = low

    def spots(i):
        start = pl.multiple_of(i * PACK, PACK)
        return pl.ds(start, PACK), pl.ds(pl.multiple_of(rows + start, PACK), PACK)

    @pl.loop(0, rows // PACK)
    def _(i):
        here, below = spots(i)
        for j in range(jblocks):
            cross = []
            for h in range(FOLD):
                b = h * jblocks + j
                cut = slice(b * LANES, (b + 1) * LANES)
                re = im = None
                for g in range(segs):
                    ra, rb = g * blocks + b, (segs + g) * blocks + b
                    sr = slab[ra // per, ra % per : ra % per + 1, :]
                    si = slab[rb // per, rb % per : rb % per + 1, :]
                    xr, xi = vals[0, g, here, cut], vals[1, g, here, cut]
                    tr, ti = sr * xr + si * xi, sr * xi - si * xr
                    re, im = (tr, ti) if re is None else (re + tr, im + ti)
                vals[0, 0, here, cut] = re
                vals[1, 0, here, cut] = im
                cross.append((re, im))
            split(even, cross, j, here, below)

    def fold_odd(i):
        here, below = spots(i)
        for j in range(jblocks):
            turned = []
            for h in range(FOLD):
                b = h * jblocks + j
                cut = slice(b * LANES, (b + 1) * LANES)
                turned.append(turn((vals[0, 0, here, cut], vals[1, 0, here, cut]), h))
            split(odd, turned, j, here, below)

    load_tab.wait()

    def give(k, d):
        to = lax.rem(win + d, nwin)
        return pltpu.make_async_remote_copy(
            src_ref=part.at[k, to], dst_ref=come.at[d - 1, k], send_sem=s3.at[k, d - 1],
            recv_sem=r3.at[k, d - 1], device_id=(chan, to), device_id_type=MESH)

    def lags(k, folded):
        r = lax.dot_general(tab[k], folded, (((1,), (1,)), ((), ())),
                            preferred_element_type=jnp.float32)
        low = r[:steps, rows:] + r[steps:, :rows] + r[steps:, rows:]
        part[k] = (r[:steps, :rows] + low).reshape(nwin, mine_steps, rows)
        for d in range(1, nwin):
            give(k, d).start()

    groups_each = rows // PACK // FOLD

    @pl.loop(0, FOLD)
    def _(m):
        lags(2 * m, even[m])
        for i in range(groups_each):
            fold_odd(m * groups_each + i)

    @pl.loop(0, FOLD)
    def _(m):
        lags(2 * m + 1, odd[m])

    for d in range(1, NEAR):
        scatter(d).wait_send()
        gather(d).wait_send()
    for d in range(1, nfar):
        across(d).wait_send()

    for k in range(CLASSES):
        value = part[k, win]
        for d in range(1, nwin):
            give(k, d).wait_recv()
            value = value + come[d - 1, k]
        acc[pl.ds(k, mine_steps, stride=CLASSES), :] = value

    for t in range(L // nwin // LANES):
        cut = slice(t * LANES, (t + 1) * LANES)
        out_ref[:, cut] = acc[cut, :].T

    @pl.loop(0, CLASSES)
    def _(k):
        for d in range(1, nwin):
            give(k, d).wait_send()


def body(spectra, exponents, source_channels):
    nch, nwin = lax.axis_size("chan"), lax.axis_size("win")
    _, segs, rows, nbin = spectra.shape
    per = 2 * segs * nbin // LANES // NEAR
    steps = L // CLASSES
    width = nbin // FOLD
    tables = jnp.asarray(lag_tables(nbin, 1.0 / math.sqrt(4.0 * nbin * segs * nwin)))
    f32, bf16, dma = jnp.float32, jnp.bfloat16, pltpu.SemaphoreType.DMA
    call = pl.pallas_call(
        functools.partial(kernel, nch, nwin),
        out_shape=jax.ShapeDtypeStruct((rows, L // nwin), f32),
        in_specs=[
            pl.BlockSpec(memory_space=pltpu.SMEM),
            pl.BlockSpec(memory_space=pl.ANY),
            pl.BlockSpec(memory_space=pl.ANY),
            pl.BlockSpec(memory_space=pl.ANY),
        ],
        out_specs=pl.BlockSpec(memory_space=pltpu.VMEM),
        scratch_shapes=[
            pltpu.VMEM(spectra.shape, bf16),
            pltpu.VMEM((CLASSES, 2 * steps, 2 * width), bf16),
            pltpu.VMEM(spectra.shape, f32),
            pltpu.VMEM((segs, nbin // LANES, rows), jnp.int32),
            pltpu.VMEM((rows, LANES), f32),
            pltpu.VMEM((NEAR, per, LANES), f32),
            pltpu.VMEM((NEAR, per, LANES), f32),
            pltpu.VMEM((per, LANES), f32),
            pltpu.VMEM((nch // NEAR, per, LANES), f32),
            pltpu.VMEM((per, LANES), f32),
            pltpu.VMEM((NEAR, per, LANES), f32),
            pltpu.VMEM((FOLD, 2 * rows, 2 * width), bf16),
            pltpu.VMEM((FOLD, 2 * rows, 2 * width), bf16),
            pltpu.VMEM((CLASSES, nwin, steps // nwin, rows), f32),
            pltpu.VMEM((nwin - 1, CLASSES, steps // nwin, rows), f32),
            pltpu.VMEM((L // nwin, rows), f32),
            dma, dma, dma,
            dma((NEAR,)), dma((NEAR,)), dma((nch // NEAR,)), dma((nch // NEAR,)), dma((NEAR,)), dma((NEAR,)),
            dma((CLASSES, nwin - 1)), dma((CLASSES, nwin - 1)),
        ],
        compiler_params=pltpu.CompilerParams(
            collective_id=0, has_side_effects=True, vmem_limit_bytes=60 * 2**20),
    )
    out = [call(source_channels[s : s + 1], jnp.swapaxes(exponents, 1, 2), spectra, tables)
           for s in range(source_channels.shape[0])]
    return jnp.stack(out)


def solution(mesh):
    return jax.shard_map(
        body,
        mesh=mesh,
        in_specs=(P(None, "win", "chan", None), P("win", "chan", None), P()),
        out_specs=P(None, "chan", "win"),
        check_vma=False,
    )
```

```python
import functools
import math

import jax
import jax.numpy as jnp
import ml_dtypes
import numpy as np
from jax import lax
from jax.experimental import pallas as pl
from jax.experimental.pallas import tpu as pltpu
from jax.sharding import PartitionSpec as P

L = 2048
FOLD = 8
CLASSES = 2 * FOLD
LANES = 128
PACK = 16
NEAR = 4
MESH = pl.DeviceIdType.MESH


def lag_tables(nbin, norm):
    width = nbin // FOLD
    steps = L // CLASSES
    tau = np.arange(CLASSES)[:, None] + CLASSES * (np.arange(steps) - steps // 2)[None, :]
    phase = (tau[:, :, None] * np.arange(width)[None, None, :]) % (2 * nbin)
    angle = phase * (2.0 * math.pi / (2 * nbin))
    full = np.concatenate([np.cos(angle), -np.sin(angle)], axis=2) * norm
    high = full.astype(np.float32).astype(ml_dtypes.bfloat16)
    low = (full - high.astype(np.float64)).astype(np.float32).astype(ml_dtypes.bfloat16)
    return np.concatenate([high, low], axis=1)


def turn(value, eighths):
    re, im = value
    k = eighths % 16
    if k == 0:
        return re, im
    if k == 4:
        return -im, re
    if k == 8:
        return -re, -im
    if k == 12:
        return im, -re
    if k == 2:
        c = math.sqrt(0.5)
        return (re - im) * c, (re + im) * c
    if k == 6:
        c = math.sqrt(0.5)
        return (re + im) * -c, (re - im) * c
    c, s = math.cos(math.pi * k / 8), math.sin(math.pi * k / 8)
    return re * c - im * s, re * s + im * c


def dft(values):
    n = len(values)
    if n == 1:
        return values
    even, odd = dft(values[0::2]), dft(values[1::2])
    odd = [turn(v, 16 // n * k) for k, v in enumerate(odd)]
    low = [(a[0] + b[0], a[1] + b[1]) for a, b in zip(even, odd)]
    high = [(a[0] - b[0], a[1] - b[1]) for a, b in zip(even, odd)]
    return low + high


def kernel(nch, nwin, src_ref, exp_hbm, spec_hbm, tab_hbm, out_ref,
           spec, tab, vals, raw, scales, pick, got, mine, got2, total, slab, even, odd,
           part, come, acc,
           spec_sem, tab_sem, exp_sem, s1, r1, s2, r2, s4, r4, s3, r3):
    chan, win = lax.axis_index("chan"), lax.axis_index("win")
    segs, rows, nbin = spec.shape[1], spec.shape[2], spec.shape[3]
    blocks = nbin // LANES
    per = slab.shape[1]
    width = nbin // FOLD
    jblocks = width // LANES
    steps = L // CLASSES
    mine_steps = steps // nwin

    load_exp = pltpu.make_async_copy(exp_hbm, raw, exp_sem)
    load_exp.start()
    loads = [
        [pltpu.make_async_copy(spec_hbm.at[plane, g], spec.at[plane, g], spec_sem.at[plane, g])
         for g in range(segs)] for plane in range(2)]
    for load in loads[0] + loads[1]:
        load.start()
    load_tab = pltpu.make_async_copy(tab_hbm, tab, tab_sem)

    near, far = lax.rem(chan, NEAR), lax.div(chan, NEAR)
    nfar = nch // NEAR

    def beside(d):
        return lax.rem(near + d, NEAR)

    def ahead(d):
        return lax.rem(far + d, nfar) * NEAR + near

    barrier = pltpu.get_barrier_semaphore()
    for d in range(1, NEAR):
        pl.semaphore_signal(barrier, inc=1, device_id=(far * NEAR + beside(d), win), device_id_type=MESH)

    @pl.loop(1, nfar)
    def _(d):
        pl.semaphore_signal(barrier, inc=1, device_id=(ahead(d), win), device_id_type=MESH)

    @pl.loop(1, nwin)
    def _(d):
        pl.semaphore_signal(barrier, inc=1, device_id=(chan, lax.rem(win + d, nwin)), device_id_type=MESH)

    load_exp.wait()
    flat = jnp.exp2(raw[...].astype(jnp.float32)).reshape(segs * blocks, rows)
    square = jnp.concatenate([flat, jnp.ones((LANES - segs * blocks, rows), jnp.float32)], axis=0)
    scales[...] = square.T
    local = src_ref[0] - chan * rows
    line = lax.broadcasted_iota(jnp.int32, (rows, LANES), 0)
    hits = (line == local).astype(jnp.float32)
    groups = rows // PACK
    marks = [hits[i * PACK : (i + 1) * PACK].astype(jnp.bfloat16) for i in range(groups)]
    def scatter(d):
        to = beside(d)
        return pltpu.make_async_remote_copy(
            src_ref=pick.at[to], dst_ref=got.at[d], send_sem=s1.at[d], recv_sem=r1.at[d],
            device_id=(far * NEAR + to, win), device_id_type=MESH)

    def send(piece):
        @pl.when(near != piece)
        def _():
            scatter(lax.rem(piece - near + NEAR, NEAR)).start()

    scale = jnp.sum(scales[...] * hits, axis=0, keepdims=True)
    sent = 0
    for plane in range(2):
        for g in range(segs):
            loads[plane][g].wait()
            for b in range(blocks):
                wide = jnp.broadcast_to(scale[:, g * blocks + b : g * blocks + b + 1], (1, LANES))
                x = None
                for i in range(groups):
                    y = spec[plane, g, i * PACK : (i + 1) * PACK, b * LANES : (b + 1) * LANES] * marks[i]
                    x = y if x is None else x + y
                row = (plane * segs + g) * blocks + b
                one = jnp.sum(x.astype(jnp.float32), axis=0, keepdims=True)
                pick[row // per, row % per : row % per + 1, :] = one * wide
            if plane == 0 and g == 0:
                pl.semaphore_wait(barrier, NEAR + nfar + nwin - 3)
            done = ((plane * segs + g) + 1) * blocks // per
            for piece in range(sent, done):
                send(piece)
            sent = done
    load_tab.start()

    def across(d):
        return pltpu.make_async_remote_copy(
            src_ref=mine, dst_ref=got2.at[d], send_sem=s2.at[d], recv_sem=r2.at[d],
            device_id=(ahead(d), win), device_id_type=MESH)

    def gather(d):
        return pltpu.make_async_remote_copy(
            src_ref=total, dst_ref=slab.at[near], send_sem=s4.at[d], recv_sem=r4.at[d],
            device_id=(far * NEAR + beside(d), win), device_id_type=MESH)

    added = pick[near]
    for d in range(1, NEAR):
        scatter(d).wait_recv()
        added = added + got[d]
    mine[...] = added
    for d in range(1, nfar):
        across(d).start()

    @pl.loop(0, rows // PACK)
    def _(i):
        here = pl.ds(pl.multiple_of(i * PACK, PACK), PACK)
        scale = scales[here, :]
        for g in range(segs):
            for b in range(blocks):
                wide = jnp.broadcast_to(scale[:, g * blocks + b : g * blocks + b + 1], (PACK, LANES))
                cut = slice(b * LANES, (b + 1) * LANES)
                for plane in range(2):
                    x = spec[plane, g, here, cut].astype(jnp.float32)
                    vals[plane, g, here, cut] = x * wide

    for d in range(1, nfar):
        across(d).wait_recv()
        added = added + got2[d]
    total[...] = added
    slab[near] = added
    for d in range(1, NEAR):
        gather(d).start()
    for d in range(1, NEAR):
        gather(d).wait_recv()

    def split(folded, pairs, j, here, below):
        for m, pair in enumerate(dft(pairs)):
            for plane in range(2):
                cut = slice(plane * width + j * LANES, plane * width + (j + 1) * LANES)
                high = pair[plane].astype(jnp.bfloat16)
                low = (pair[plane] - high.astype(jnp.float32)).astype(jnp.bfloat16)
                folded[m, here, cut] = high
                folded[m, below, cut] = low

    def spots(i):
        start = pl.multiple_of(i * PACK, PACK)
        return pl.ds(start, PACK), pl.ds(pl.multiple_of(rows + start, PACK), PACK)

    @pl.loop(0, rows // PACK)
    def _(i):
        here, below = spots(i)
        for j in range(jblocks):
            cross = []
            for h in range(FOLD):
                b = h * jblocks + j
                cut = slice(b * LANES, (b + 1) * LANES)
                re = im = None
                for g in range(segs):
                    ra, rb = g * blocks + b, (segs + g) * blocks + b
                    sr = slab[ra // per, ra % per : ra % per + 1, :]
                    si = slab[rb // per, rb % per : rb % per + 1, :]
                    xr, xi = vals[0, g, here, cut], vals[1, g, here, cut]
                    tr, ti = sr * xr + si * xi, sr * xi - si * xr
                    re, im = (tr, ti) if re is None else (re + tr, im + ti)
                vals[0, 0, here, cut] = re
                vals[1, 0, here, cut] = im
                cross.append((re, im))
            split(even, cross, j, here, below)

    def fold_odd(i):
        here, below = spots(i)
        for j in range(jblocks):
            turned = []
            for h in range(FOLD):
                b = h * jblocks + j
                cut = slice(b * LANES, (b + 1) * LANES)
                turned.append(turn((vals[0, 0, here, cut], vals[1, 0, here, cut]), h))
            split(odd, turned, j, here, below)

    load_tab.wait()

    def give(k, d):
        to = lax.rem(win + d, nwin)
        return pltpu.make_async_remote_copy(
            src_ref=part.at[k, to], dst_ref=come.at[d - 1, k], send_sem=s3.at[k, d - 1],
            recv_sem=r3.at[k, d - 1], device_id=(chan, to), device_id_type=MESH)

    def lags(k, folded):
        r = lax.dot_general(tab[k], folded, (((1,), (1,)), ((), ())),
                            preferred_element_type=jnp.float32)
        low = r[:steps, rows:] + r[steps:, :rows] + r[steps:, rows:]
        part[k] = (r[:steps, :rows] + low).reshape(nwin, mine_steps, rows)
        for d in range(1, nwin):
            give(k, d).start()

    groups_each = rows // PACK // FOLD

    @pl.loop(0, FOLD)
    def _(m):
        lags(2 * m, even[m])
        for i in range(groups_each):
            fold_odd(m * groups_each + i)

    @pl.loop(0, FOLD)
    def _(m):
        lags(2 * m + 1, odd[m])

    for d in range(1, NEAR):
        scatter(d).wait_send()
        gather(d).wait_send()
    for d in range(1, nfar):
        across(d).wait_send()

    for k in range(CLASSES):
        value = part[k, win]
        for d in range(1, nwin):
            give(k, d).wait_recv()
            value = value + come[d - 1, k]
        acc[pl.ds(k, mine_steps, stride=CLASSES), :] = value

    for t in range(L // nwin // LANES):
        cut = slice(t * LANES, (t + 1) * LANES)
        out_ref[:, cut] = acc[cut, :].T

    @pl.loop(0, CLASSES)
    def _(k):
        for d in range(1, nwin):
            give(k, d).wait_send()


def body(spectra, exponents, source_channels):
    nch, nwin = lax.axis_size("chan"), lax.axis_size("win")
    _, segs, rows, nbin = spectra.shape
    per = 2 * segs * nbin // LANES // NEAR
    steps = L // CLASSES
    width = nbin // FOLD
    tables = jnp.asarray(lag_tables(nbin, 1.0 / math.sqrt(4.0 * nbin * segs * nwin)))
    f32, bf16, dma = jnp.float32, jnp.bfloat16, pltpu.SemaphoreType.DMA
    call = pl.pallas_call(
        functools.partial(kernel, nch, nwin),
        out_shape=jax.ShapeDtypeStruct((rows, L // nwin), f32),
        in_specs=[
            pl.BlockSpec(memory_space=pltpu.SMEM),
            pl.BlockSpec(memory_space=pl.ANY),
            pl.BlockSpec(memory_space=pl.ANY),
            pl.BlockSpec(memory_space=pl.ANY),
        ],
        out_specs=pl.BlockSpec(memory_space=pltpu.VMEM),
        scratch_shapes=[
            pltpu.VMEM(spectra.shape, bf16),
            pltpu.VMEM((CLASSES, 2 * steps, 2 * width), bf16),
            pltpu.VMEM(spectra.shape, f32),
            pltpu.VMEM((segs, nbin // LANES, rows), jnp.int32),
            pltpu.VMEM((rows, LANES), f32),
            pltpu.VMEM((NEAR, per, LANES), f32),
            pltpu.VMEM((NEAR, per, LANES), f32),
            pltpu.VMEM((per, LANES), f32),
            pltpu.VMEM((nch // NEAR, per, LANES), f32),
            pltpu.VMEM((per, LANES), f32),
            pltpu.VMEM((NEAR, per, LANES), f32),
            pltpu.VMEM((FOLD, 2 * rows, 2 * width), bf16),
            pltpu.VMEM((FOLD, 2 * rows, 2 * width), bf16),
            pltpu.VMEM((CLASSES, nwin, steps // nwin, rows), f32),
            pltpu.VMEM((nwin - 1, CLASSES, steps // nwin, rows), f32),
            pltpu.VMEM((L // nwin, rows), f32),
            dma((2, segs)), dma, dma,
            dma((NEAR,)), dma((NEAR,)), dma((nch // NEAR,)), dma((nch // NEAR,)), dma((NEAR,)), dma((NEAR,)),
            dma((CLASSES, nwin - 1)), dma((CLASSES, nwin - 1)),
        ],
        compiler_params=pltpu.CompilerParams(
            collective_id=0, has_side_effects=True, vmem_limit_bytes=60 * 2**20),
    )
    out = [call(source_channels[s : s + 1], jnp.swapaxes(exponents, 1, 2), spectra, tables)
           for s in range(source_channels.shape[0])]
    return jnp.stack(out)


def solution(mesh):
    return jax.shard_map(
        body,
        mesh=mesh,
        in_specs=(P(None, "win", "chan", None), P("win", "chan", None), P()),
        out_specs=P(None, "chan", "win"),
        check_vma=False,
    )
```

```python
import functools
import math

import jax
import jax.numpy as jnp
import ml_dtypes
import numpy as np
from jax import lax
from jax.experimental import pallas as pl
from jax.experimental.pallas import tpu as pltpu
from jax.sharding import PartitionSpec as P

L = 2048
FOLD = 8
CLASSES = 2 * FOLD
LANES = 128
PACK = 16
NEAR = 4
MESH = pl.DeviceIdType.MESH


def lag_tables(nbin, norm):
    width = nbin // FOLD
    steps = L // CLASSES
    tau = np.arange(CLASSES)[:, None] + CLASSES * (np.arange(steps) - steps // 2)[None, :]
    phase = (tau[:, :, None] * np.arange(width)[None, None, :]) % (2 * nbin)
    angle = phase * (2.0 * math.pi / (2 * nbin))
    full = np.concatenate([np.cos(angle), -np.sin(angle)], axis=2) * norm
    high = full.astype(np.float32).astype(ml_dtypes.bfloat16)
    low = (full - high.astype(np.float64)).astype(np.float32).astype(ml_dtypes.bfloat16)
    return np.concatenate([high, low], axis=1)


def turn(value, eighths):
    re, im = value
    k = eighths % 16
    if k == 0:
        return re, im
    if k == 4:
        return -im, re
    if k == 8:
        return -re, -im
    if k == 12:
        return im, -re
    if k == 2:
        c = math.sqrt(0.5)
        return (re - im) * c, (re + im) * c
    if k == 6:
        c = math.sqrt(0.5)
        return (re + im) * -c, (re - im) * c
    c, s = math.cos(math.pi * k / 8), math.sin(math.pi * k / 8)
    return re * c - im * s, re * s + im * c


def dft(values):
    n = len(values)
    if n == 1:
        return values
    even, odd = dft(values[0::2]), dft(values[1::2])
    odd = [turn(v, 16 // n * k) for k, v in enumerate(odd)]
    low = [(a[0] + b[0], a[1] + b[1]) for a, b in zip(even, odd)]
    high = [(a[0] - b[0], a[1] - b[1]) for a, b in zip(even, odd)]
    return low + high


def kernel(nch, nwin, src_ref, exp_hbm, spec_hbm, tab_hbm, out_ref,
           spec, tab, vals, raw, scales, pick, got, mine, got2, total, slab, even, odd,
           part, come,
           spec_sem, tab_sem, exp_sem, s1, r1, s2, r2, s4, r4, s3, r3):
    chan, win = lax.axis_index("chan"), lax.axis_index("win")
    segs, rows, nbin = spec.shape[1], spec.shape[2], spec.shape[3]
    blocks = nbin // LANES
    per = slab.shape[1]
    width = nbin // FOLD
    jblocks = width // LANES
    steps = L // CLASSES
    mine_steps = steps // nwin

    load_exp = pltpu.make_async_copy(exp_hbm, raw, exp_sem)
    load_exp.start()
    loads = [
        [pltpu.make_async_copy(spec_hbm.at[plane, g], spec.at[plane, g], spec_sem.at[plane, g])
         for g in range(segs)] for plane in range(2)]
    for load in loads[0] + loads[1]:
        load.start()
    load_tab = pltpu.make_async_copy(tab_hbm, tab, tab_sem)

    near, far = lax.rem(chan, NEAR), lax.div(chan, NEAR)
    nfar = nch // NEAR

    def beside(d):
        return lax.rem(near + d, NEAR)

    def ahead(d):
        return lax.rem(far + d, nfar) * NEAR + near

    barrier = pltpu.get_barrier_semaphore()
    for d in range(1, NEAR):
        pl.semaphore_signal(barrier, inc=1, device_id=(far * NEAR + beside(d), win), device_id_type=MESH)

    @pl.loop(1, nfar)
    def _(d):
        pl.semaphore_signal(barrier, inc=1, device_id=(ahead(d), win), device_id_type=MESH)

    @pl.loop(1, nwin)
    def _(d):
        pl.semaphore_signal(barrier, inc=1, device_id=(chan, lax.rem(win + d, nwin)), device_id_type=MESH)

    load_exp.wait()
    flat = jnp.exp2(raw[...].astype(jnp.float32)).reshape(segs * blocks, rows)
    square = jnp.concatenate([flat, jnp.ones((LANES - segs * blocks, rows), jnp.float32)], axis=0)
    scales[...] = square.T
    local = src_ref[0] - chan * rows
    line = lax.broadcasted_iota(jnp.int32, (rows, LANES), 0)
    hits = (line == local).astype(jnp.float32)
    groups = rows // PACK
    marks = [hits[i * PACK : (i + 1) * PACK].astype(jnp.bfloat16) for i in range(groups)]
    def scatter(d):
        to = beside(d)
        return pltpu.make_async_remote_copy(
            src_ref=pick.at[to], dst_ref=got.at[d], send_sem=s1.at[d], recv_sem=r1.at[d],
            device_id=(far * NEAR + to, win), device_id_type=MESH)

    def send(piece):
        @pl.when(near != piece)
        def _():
            scatter(lax.rem(piece - near + NEAR, NEAR)).start()

    scale = jnp.sum(scales[...] * hits, axis=0, keepdims=True)
    sent = 0
    for plane in range(2):
        for g in range(segs):
            loads[plane][g].wait()
            for b in range(blocks):
                wide = jnp.broadcast_to(scale[:, g * blocks + b : g * blocks + b + 1], (1, LANES))
                x = None
                for i in range(groups):
                    y = spec[plane, g, i * PACK : (i + 1) * PACK, b * LANES : (b + 1) * LANES] * marks[i]
                    x = y if x is None else x + y
                row = (plane * segs + g) * blocks + b
                one = jnp.sum(x.astype(jnp.float32), axis=0, keepdims=True)
                pick[row // per, row % per : row % per + 1, :] = one * wide
            if plane == 0 and g == 0:
                pl.semaphore_wait(barrier, NEAR + nfar + nwin - 3)
            done = ((plane * segs + g) + 1) * blocks // per
            for piece in range(sent, done):
                send(piece)
            sent = done
    load_tab.start()

    def across(d):
        return pltpu.make_async_remote_copy(
            src_ref=mine, dst_ref=got2.at[d], send_sem=s2.at[d], recv_sem=r2.at[d],
            device_id=(ahead(d), win), device_id_type=MESH)

    def gather(d):
        return pltpu.make_async_remote_copy(
            src_ref=total, dst_ref=slab.at[near], send_sem=s4.at[d], recv_sem=r4.at[d],
            device_id=(far * NEAR + beside(d), win), device_id_type=MESH)

    added = pick[near]
    for d in range(1, NEAR):
        scatter(d).wait_recv()
        added = added + got[d]
    mine[...] = added
    for d in range(1, nfar):
        across(d).start()

    @pl.loop(0, rows // PACK)
    def _(i):
        here = pl.ds(pl.multiple_of(i * PACK, PACK), PACK)
        scale = scales[here, :]
        for g in range(segs):
            for b in range(blocks):
                wide = jnp.broadcast_to(scale[:, g * blocks + b : g * blocks + b + 1], (PACK, LANES))
                cut = slice(b * LANES, (b + 1) * LANES)
                for plane in range(2):
                    x = spec[plane, g, here, cut].astype(jnp.float32)
                    vals[plane, g, here, cut] = x * wide

    for d in range(1, nfar):
        across(d).wait_recv()
        added = added + got2[d]
    total[...] = added
    slab[near] = added
    for d in range(1, NEAR):
        gather(d).start()
    for d in range(1, NEAR):
        gather(d).wait_recv()

    def split(folded, pairs, j, here, below):
        for m, pair in enumerate(dft(pairs)):
            for plane in range(2):
                cut = slice(plane * width + j * LANES, plane * width + (j + 1) * LANES)
                high = pair[plane].astype(jnp.bfloat16)
                low = (pair[plane] - high.astype(jnp.float32)).astype(jnp.bfloat16)
                folded[m, here, cut] = high
                folded[m, below, cut] = low

    def spots(i):
        start = pl.multiple_of(i * PACK, PACK)
        return pl.ds(start, PACK), pl.ds(pl.multiple_of(rows + start, PACK), PACK)

    @pl.loop(0, rows // PACK)
    def _(i):
        here, below = spots(i)
        for j in range(jblocks):
            cross = []
            for h in range(FOLD):
                b = h * jblocks + j
                cut = slice(b * LANES, (b + 1) * LANES)
                re = im = None
                for g in range(segs):
                    ra, rb = g * blocks + b, (segs + g) * blocks + b
                    sr = slab[ra // per, ra % per : ra % per + 1, :]
                    si = slab[rb // per, rb % per : rb % per + 1, :]
                    xr, xi = vals[0, g, here, cut], vals[1, g, here, cut]
                    tr, ti = sr * xr + si * xi, sr * xi - si * xr
                    re, im = (tr, ti) if re is None else (re + tr, im + ti)
                vals[0, 0, here, cut] = re
                vals[1, 0, here, cut] = im
                cross.append((re, im))
            split(even, cross, j, here, below)

    def fold_odd(i):
        here, below = spots(i)
        for j in range(jblocks):
            turned = []
            for h in range(FOLD):
                b = h * jblocks + j
                cut = slice(b * LANES, (b + 1) * LANES)
                turned.append(turn((vals[0, 0, here, cut], vals[1, 0, here, cut]), h))
            split(odd, turned, j, here, below)

    load_tab.wait()

    def give(k, d):
        to = lax.rem(win + d, nwin)
        return pltpu.make_async_remote_copy(
            src_ref=part.at[k, to], dst_ref=come.at[d - 1, k], send_sem=s3.at[k, d - 1],
            recv_sem=r3.at[k, d - 1], device_id=(chan, to), device_id_type=MESH)

    def lags(k, folded):
        r = lax.dot_general(tab[k], folded, (((1,), (1,)), ((), ())),
                            preferred_element_type=jnp.float32)
        low = r[:steps, rows:] + r[steps:, :rows] + r[steps:, rows:]
        part[k] = (r[:steps, :rows] + low).reshape(nwin, mine_steps, rows)
        for d in range(1, nwin):
            give(k, d).start()

    groups_each = rows // PACK // FOLD

    @pl.loop(0, FOLD)
    def _(m):
        lags(2 * m, even[m])
        for i in range(groups_each):
            fold_odd(m * groups_each + i)

    @pl.loop(0, FOLD)
    def _(m):
        lags(2 * m + 1, odd[m])

    for d in range(1, NEAR):
        scatter(d).wait_send()
        gather(d).wait_send()
    for d in range(1, nfar):
        across(d).wait_send()

    for k in range(CLASSES):
        value = part[k, win]
        for d in range(1, nwin):
            give(k, d).wait_recv()
            value = value + come[d - 1, k]
        out_ref[pl.ds(k, mine_steps, stride=CLASSES), :] = value

    @pl.loop(0, CLASSES)
    def _(k):
        for d in range(1, nwin):
            give(k, d).wait_send()


def body(spectra, exponents, source_channels):
    nch, nwin = lax.axis_size("chan"), lax.axis_size("win")
    _, segs, rows, nbin = spectra.shape
    per = 2 * segs * nbin // LANES // NEAR
    steps = L // CLASSES
    width = nbin // FOLD
    tables = jnp.asarray(lag_tables(nbin, 1.0 / math.sqrt(4.0 * nbin * segs * nwin)))
    f32, bf16, dma = jnp.float32, jnp.bfloat16, pltpu.SemaphoreType.DMA
    call = pl.pallas_call(
        functools.partial(kernel, nch, nwin),
        out_shape=jax.ShapeDtypeStruct((L // nwin, rows), f32),
        in_specs=[
            pl.BlockSpec(memory_space=pltpu.SMEM),
            pl.BlockSpec(memory_space=pl.ANY),
            pl.BlockSpec(memory_space=pl.ANY),
            pl.BlockSpec(memory_space=pl.ANY),
        ],
        out_specs=pl.BlockSpec(memory_space=pltpu.VMEM),
        scratch_shapes=[
            pltpu.VMEM(spectra.shape, bf16),
            pltpu.VMEM((CLASSES, 2 * steps, 2 * width), bf16),
            pltpu.VMEM(spectra.shape, f32),
            pltpu.VMEM((segs, nbin // LANES, rows), jnp.int32),
            pltpu.VMEM((rows, LANES), f32),
            pltpu.VMEM((NEAR, per, LANES), f32),
            pltpu.VMEM((NEAR, per, LANES), f32),
            pltpu.VMEM((per, LANES), f32),
            pltpu.VMEM((nch // NEAR, per, LANES), f32),
            pltpu.VMEM((per, LANES), f32),
            pltpu.VMEM((NEAR, per, LANES), f32),
            pltpu.VMEM((FOLD, 2 * rows, 2 * width), bf16),
            pltpu.VMEM((FOLD, 2 * rows, 2 * width), bf16),
            pltpu.VMEM((CLASSES, nwin, steps // nwin, rows), f32),
            pltpu.VMEM((nwin - 1, CLASSES, steps // nwin, rows), f32),
            dma((2, segs)), dma, dma,
            dma((NEAR,)), dma((NEAR,)), dma((nch // NEAR,)), dma((nch // NEAR,)), dma((NEAR,)), dma((NEAR,)),
            dma((CLASSES, nwin - 1)), dma((CLASSES, nwin - 1)),
        ],
        compiler_params=pltpu.CompilerParams(
            collective_id=0, has_side_effects=True, vmem_limit_bytes=60 * 2**20),
    )
    out = [call(source_channels[s : s + 1], jnp.swapaxes(exponents, 1, 2), spectra, tables)
           for s in range(source_channels.shape[0])]
    return jnp.stack([lagged.T for lagged in out])


def solution(mesh):
    return jax.shard_map(
        body,
        mesh=mesh,
        in_specs=(P(None, "win", "chan", None), P("win", "chan", None), P()),
        out_specs=P(None, "chan", "win"),
        check_vma=False,
    )
```
